256 devices in a mesh: gx: 16 (over z, y_lo), gy: 16 (over x, y_hi, core).
Axes of the slice: x: 4, y: 4 (y_hi: 2, y_lo: 2; y = y_hi * 2 + y_lo), z: 8, core: 2. Of those that a mesh axis runs over, the one named last changes fastest.
Arguments:
- face_matrix: float32 [16, 64, 256, 256], P('gx', 'gy')
- couple_x: float32 [16, 64, 256, 256], P('gx', 'gy')
- couple_y: float32 [16, 64, 256, 256], P('gx', 'gy')
- skeleton: int32 [16, 64, 96], P('gx', 'gy'), may hold values from 0 to 255, as said below
- redundant: int32 [16, 64, 160], P('gx', 'gy'), may hold values from 0 to 255, as said below
Outputs:
- face_block: float32 [16, 64, 256, 256], P('gx', 'gy')
- skeleton_block: float32 [16, 64, 96, 96], P('gx', 'gy')
The draws below stay inside these ranges and needn't reach their ends.
Inputs may be any that keep to these rules, and one draw needn't show every extreme that they name: For every face, skeleton and redundant together name each of its 256 points exactly once, each list ascending. `redundant`: the complement of skeleton on each face, ascending.
All inputs are finite; a program needn't handle non-finite values.
Results may differ from the reference program's by a relative error of at most 0.0003.
Values sent between devices are 32-bit elements; how exact they have to be, the bound alone decides.
No kernel may reach another device: no remote copies, remote signals or barrier semaphores. Data moves between devices by JAX's collectives and lax.ppermute only.
A program may use at most 64 MiB of HBM per device.

```python
import math
import jax
import jax.numpy as jnp
from jax import lax

F = 256
S = 96
NXF = 16
NYF = 64


def split_points(key):
    scores = jax.random.randint(key, (NXF, NYF, F), 0, 2 ** 20) * F + jnp.arange(F, dtype=jnp.int32)
    order = jnp.argsort(scores, axis=-1).astype(jnp.int32)
    return (jnp.sort(order[..., :S], axis=-1), jnp.sort(order[..., S:], axis=-1))


def draw_skeleton(key, part):
    chosen, others = split_points(key)
    return chosen


def draw_redundant(key, part):
    chosen, others = split_points(key)
    return others


def face_points():
    side = max(math.isqrt(F), 1)
    index = jnp.arange(F, dtype=jnp.int32)
    across = ((index % side).astype(jnp.float32) + 0.5) / side
    along = ((index // side).astype(jnp.float32) + 0.5) / side
    return (across, along)


def coupling(key, offset, spacing, lowest, highest_scale):
    row_key, col_key = jax.random.split(key)
    across, along = face_points()
    delta_u = across[:, None] - across[None, :] - offset
    delta_v = along[:, None] - along[None, :]
    kernel = 1.0 / jnp.sqrt(delta_u * delta_u + delta_v * delta_v + spacing * spacing)
    row_scale = jnp.exp(jax.random.uniform(row_key, (NXF, NYF, F, 1), jnp.float32, math.log(lowest), math.log(highest_scale)))
    col_scale = jnp.exp(jax.random.uniform(col_key, (NXF, NYF, 1, F), jnp.float32, math.log(lowest), math.log(highest_scale)))
    return 0.09 * row_scale * col_scale * kernel


def draw_couple_x(key, part):
    key = jax.random.fold_in(key, 21)
    smooth_key, noise_key = jax.random.split(key)
    smooth = coupling(smooth_key, 0.0, 1.0, 0.5, 2.0)
    noise = jax.random.normal(noise_key, (NXF, NYF, F, F), jnp.float32) * 0.025
    return smooth + noise


def draw_couple_y(key, part):
    key = jax.random.fold_in(key, 22)
    smooth_key, noise_key = jax.random.split(key)
    smooth = coupling(smooth_key, 1.0, 0.5, 0.5, 2.0)
    noise = jax.random.normal(noise_key, (NXF, NYF, F, F), jnp.float32) * 0.025
    return smooth + noise


def draw_face_matrix(key, part):
    key = jax.random.fold_in(key, 11)
    gain_key, diag_key = jax.random.split(key)
    across, along = face_points()
    delta_u = across[:, None] - across[None, :]
    delta_v = along[:, None] - along[None, :]
    kernel = jnp.exp(-jnp.sqrt(delta_u * delta_u + delta_v * delta_v) / 0.2)
    gain = jnp.exp(jax.random.uniform(gain_key, (NXF, NYF, F), jnp.float32, math.log(0.6), math.log(1.6)))
    diagonal = jax.random.uniform(diag_key, (NXF, NYF, F), jnp.float32, 0.15, 0.4)
    return gain[..., :, None] * gain[..., None, :] * kernel + jnp.eye(F, dtype=jnp.float32) * diagonal[..., None]


def setup_inputs(seed: int = 0) -> dict:
    splits = jax.random.split(jax.random.key(seed), 6)
    face_matrix = draw_face_matrix(jax.random.fold_in(splits[5], 71), 0)
    couple_x = draw_couple_x(jax.random.fold_in(splits[5], 71), 0)
    couple_y = draw_couple_y(jax.random.fold_in(splits[5], 71), 0)
    skeleton = draw_skeleton(jax.random.fold_in(splits[5], 71), 0)
    redundant = draw_redundant(jax.random.fold_in(splits[5], 71), 0)
    return {"face_matrix": face_matrix, "couple_x": couple_x, "couple_y": couple_y, "skeleton": skeleton, "redundant": redundant}


def skeletonize(face_mat, beside_all, skel_idx, red_idx):
    highest = lax.Precision.HIGHEST
    near_skel = jnp.take(beside_all, skel_idx, axis=0)
    near_red = jnp.take(beside_all, red_idx, axis=0)
    gram_mat = jnp.dot(near_skel, near_skel.T, precision=highest)
    cross_mat = jnp.dot(near_skel, near_red.T, precision=highest)
    gram_factor = jnp.linalg.cholesky(gram_mat)
    interp = jax.scipy.linalg.cho_solve((gram_factor, True), cross_mat)
    residual_rows = near_red - jnp.dot(interp.T, near_skel, precision=highest)
    skel_rows = jnp.take(face_mat, skel_idx, axis=0)
    red_rows = jnp.take(face_mat, red_idx, axis=0)
    skel_skel = jnp.take(skel_rows, skel_idx, axis=1)
    skel_red = jnp.take(skel_rows, red_idx, axis=1)
    red_red = jnp.take(red_rows, red_idx, axis=1)
    red_skel_new = skel_red.T - jnp.dot(interp.T, skel_skel, precision=highest)
    red_red_new = red_red - jnp.dot(interp.T, skel_red, precision=highest) - jnp.dot(red_skel_new, interp, precision=highest)
    lower_factor = jnp.linalg.cholesky(red_red_new)
    solved = jax.scipy.linalg.solve_triangular(lower_factor, red_skel_new, lower=True)
    factors = jax.scipy.linalg.solve_triangular(lower_factor, residual_rows, lower=True)
    skel_out = skel_skel - jnp.dot(solved.T, solved, precision=highest)
    return (skel_out, factors)

def gram_of(pieces):
    return jnp.einsum('...rf,...rg->...fg', pieces, pieces, precision=lax.Precision.HIGHEST)

def reference(face_matrix, couple_x, couple_y, skeleton, redundant):
    prev_y = jnp.roll(couple_y, 1, axis=1)

    def row_step(carried, row_index):
        before = (row_index + NXF - 1) % NXF
        face_rows = lax.dynamic_index_in_dim(face_matrix, row_index, 0, keepdims=False)
        here_x = lax.dynamic_index_in_dim(couple_x, row_index, 0, keepdims=False)
        back_x = lax.dynamic_index_in_dim(couple_x, before, 0, keepdims=False)
        here_y = lax.dynamic_index_in_dim(couple_y, row_index, 0, keepdims=False)
        back_y = lax.dynamic_index_in_dim(prev_y, row_index, 0, keepdims=False)
        beside_all = jnp.concatenate([here_x, jnp.swapaxes(back_x, -1, -2), here_y, jnp.swapaxes(back_y, -1, -2)], axis=-1)
        skel_now = lax.dynamic_index_in_dim(skeleton, row_index, 0, keepdims=False)
        red_now = lax.dynamic_index_in_dim(redundant, row_index, 0, keepdims=False)
        skel_row, factors = jax.vmap(skeletonize)(face_rows, beside_all, skel_now, red_now)
        plus_x = gram_of(factors[..., 0:F])
        minus_x = gram_of(factors[..., F:2 * F])
        plus_y = gram_of(factors[..., 2 * F:3 * F])
        minus_y = gram_of(factors[..., 3 * F:4 * F])
        from_below = jnp.roll(plus_y, 1, axis=0)
        from_above = jnp.roll(minus_y, -1, axis=0)
        partial_row = face_rows - (carried + from_below + from_above)
        return (plus_x, (partial_row, minus_x, skel_row))
    start = jnp.zeros((NYF, F, F), jnp.float32)
    last_plus, stacked = lax.scan(row_step, start, jnp.arange(NXF, dtype=jnp.int32))
    partial_all, minus_all, skeleton_block = stacked
    face_block = partial_all - jnp.roll(minus_all, -1, axis=0)
    face_block = face_block.at[0].add(-last_plus)
    return (face_block, skeleton_block)
```

```python
import jax
import jax.numpy as jnp
from jax import lax
from jax.experimental import pallas as pl
from jax.experimental.pallas import tpu as pltpu
from jax.sharding import PartitionSpec as P

F = 256
S = 96
R = 160
B = 32
NF = 4
f32 = jnp.float32
bf16 = jnp.bfloat16
HI = lax.Precision.HIGHEST


def nn(a, b):
    return lax.dot_general(a, b, (((1,), (0,)), ((), ())), precision=HI, preferred_element_type=f32)


def nt(a, b):
    return lax.dot_general(a, b, (((1,), (1,)), ((), ())), precision=HI, preferred_element_type=f32)


def split3(x):
    hi = x.astype(bf16)
    rest = x - hi.astype(f32)
    mid = rest.astype(bf16)
    low = (rest - mid.astype(f32)).astype(bf16)
    return hi, mid, low


def pick(dot, x, onehot):
    hi, mid, low = split3(x)
    return dot(hi, onehot) + dot(mid, onehot) + dot(low, onehot)


def nn16(a, b):
    return lax.dot_general(a, b, (((1,), (0,)), ((), ())), preferred_element_type=f32)


def nt16(a, b):
    return lax.dot_general(a, b, (((1,), (1,)), ((), ())), preferred_element_type=f32)


def inverse_factor(d):
    lane = lax.broadcasted_iota(jnp.int32, (8, 128), 1)
    sub = lax.broadcasted_iota(jnp.int32, (8, 128), 0)
    base = lane - lax.rem(lane, B)
    inner = lane - base
    dv = [d[8 * v : 8 * v + 8] for v in range(4)]
    ev = [jnp.where(inner == sub + 8 * v, 1.0, 0.0).astype(f32) for v in range(4)]

    def row(x, j):
        return jnp.broadcast_to(x[j : j + 1, :], (8, 128))

    out = []
    for s in range(4):
        cols = {}
        for j in range(8):
            index = base + (8 * s + j)
            for v in range(s, 4):
                cols[j, v] = jnp.take_along_axis(dv[v], index, axis=1)
        scale = jnp.ones((8, 128), f32)
        for j in range(8):
            pivot = row(cols[j, s], j)
            recip = 1.0 / pivot
            row_d = row(dv[s], j)
            row_e = row(ev[s], j)
            heads = {jj: row(cols[j, s], jj) for jj in range(j + 1, 8)}
            for v in range(s, 4):
                mult = cols[j, v] * recip
                if v == s:
                    mult = jnp.where(sub > j, mult, 0.0)
                for jj in range(j + 1, 8):
                    cols[jj, v] = cols[jj, v] - mult * heads[jj]
                dv[v] = dv[v] - mult * row_d
                ev[v] = ev[v] - mult * row_e
            scale = jnp.where(sub == j, pivot, scale)
        root = lax.rsqrt(scale)
        root = root * (1.5 - 0.5 * scale * root * root)
        out.append(ev[s] * root)
    return jnp.concatenate(out, axis=0)


def spread(x, offset):
    lane = lax.broadcasted_iota(jnp.int32, (B, 128), 1)
    rows = []
    for g in range(NF):
        piece = x[B * g : B * g + B]
        shift = (B * g - offset) % 128
        if shift:
            piece = pltpu.roll(piece, shift, 1)
        rows.append(jnp.where((lane >= B * g) & (lane < B * g + B), piece, 0.0))
    return rows


def eliminate(blocks, first):
    lane = lax.broadcasted_iota(jnp.int32, (B, 128), 1)
    count = len(blocks)
    blocks = list(blocks)
    for k in range(count):
        at = first + B * k
        tile = slice(at // 128 * 128, at // 128 * 128 + 128)
        diag = spread(blocks[k][:, tile], at % 128)
        inv = inverse_factor(diag[0] + diag[1] + diag[2] + diag[3])
        inv_bd = jnp.concatenate(
            [jnp.where((lane >= B * g) & (lane < B * g + B), inv, 0.0) for g in range(NF)], axis=0
        )
        if k + 1 < count:
            below = jnp.concatenate(
                [r for i in range(k + 1, count) for r in spread(blocks[i][:, tile], at % 128)], axis=0
            )
            lower = nt(below, inv_bd)
        top = nn(inv_bd, blocks[k])
        blocks[k] = top
        if k + 1 < count:
            step = nn(lower, top)
            for i in range(k + 1, count):
                blocks[i] = blocks[i] - step[128 * (i - k - 1) : 128 * (i - k)]
    return blocks


def stack(faces, i):
    return jnp.concatenate([x[B * i : B * i + B] for x in faces], axis=0)


def unstack(blocks, g):
    return jnp.concatenate([b[B * g : B * g + B] for b in blocks], axis=0)


def first_kernel(cx, cy, cxt, cyt, gx, gy):
    for f in range(NF):
        cxt[f] = cx[f].T
        gx[f] = nt(cxt[f], cxt[f])
    for f in range(NF):
        cyt[f] = cy[f].T
        gy[f] = nt(cyt[f], cyt[f])


def local_kernel(cx, cy, gy, k_out):
    for f in range(NF):
        k = nt(cx[f], cx[f]) + nt(cy[f], cy[f])
        if f:
            k = k + gy[f - 1]
        k_out[f] = k


def main_kernel(a, k_ref, gx, gy, perm, cxt, cyt, v_out, px_out, py_out, sk_out, q_s, ap_s, j_s):
    big = lax.broadcasted_iota(jnp.int32, (F, F), 1)
    rows3 = []
    for f in range(NF):
        wide = jnp.broadcast_to(perm[f].astype(f32), (128, F))
        column = jnp.concatenate([wide[:, :128].T, wide[:, 128:].T], axis=0)
        column = jnp.concatenate([column, column], axis=1)
        q = jnp.where(column == big.astype(f32), 1.0, 0.0).astype(bf16)
        q_s[f] = q
        k = k_ref[f] + gx[f]
        if f == 0:
            k = k + gy[0]
        half = pick(lambda x, o: nt16(x, o), k, q)
        hi, mid, low = split3(half)
        kp = nn16(q, hi) + nn16(q, mid) + nn16(q, low)
        rows3.append(kp)
        half = pick(lambda x, o: nt16(x, o), a[f], q)
        hi, mid, low = split3(half)
        ap_s[f] = nn16(q, hi) + nn16(q, mid) + nn16(q, low)
    row = lax.broadcasted_iota(jnp.int32, (S, F), 0)
    lane = lax.broadcasted_iota(jnp.int32, (S, F), 1)
    grams = [jnp.where(lane < 128, kp[:S], jnp.where(lane == row + 128, 1.0, 0.0)) for kp in rows3]
    done = eliminate([stack(grams, i) for i in range(S // B)], 0)
    tall_row = lax.broadcasted_iota(jnp.int32, (R, F), 0)
    tall_lane = lax.broadcasted_iota(jnp.int32, (R, F), 1)
    systems = []
    for f in range(NF):
        inv = unstack(done, f)[:, 128 : 128 + S]
        kps = rows3[f][S:, :S]
        jr = nn(nt(kps, inv), inv)
        xr = ap_s[f, S:, :] - nn(jr, ap_s[f, :S, :])
        t = xr[:, :S]
        right = nt(t, jr)
        tr = jnp.concatenate([t, xr[:, S:] - right], axis=1)
        hi, mid, low = split3(jr)
        qs = q_s[f, :S, :]
        y = q_s[f, S:, :].astype(f32) - (nn16(hi, qs) + nn16(mid, qs) + nn16(low, qs))
        systems.append(jnp.concatenate([tr, y], axis=1))
    done = eliminate([stack(systems, i) for i in range(R // B)], S)
    for f in range(NF):
        z = unstack(done, f)
        solved = z[:, :S]
        v = z[:, F:]
        v_out[f] = v
        ss = ap_s[f, :S, :S]
        st = z[:, :128].T[:S]
        sk_out[f] = ss - nn(st, solved)
        pt = nt(cxt[f], v)
        px_out[f] = nt(pt, pt)
        pt = nt(cyt[f], v)
        py_out[f] = nt(pt, pt)


def own_kernel(a, cy, v, py, out):
    for f in range(NF):
        x = a[f]
        if f:
            x = x - py[f - 1]
        if f + 1 < NF:
            pt = nt(cy[f], v[f + 1])
            x = x - nt(pt, pt)
        out[f] = x


def last_kernel(part, cx, cy_last, vx, vy, px, py, out):
    for f in range(NF):
        pt = nt(cx[f], vx[f])
        x = part[f] - px[f] - nt(pt, pt)
        if f == 0:
            x = x - py[0]
        if f + 1 == NF:
            pt = nt(cy_last[0], vy[0])
            x = x - nt(pt, pt)
        out[f] = x


def call(body, outs, scratch=(), flops=1_000_000_000):
    return pl.pallas_call(
        body,
        out_shape=outs,
        scratch_shapes=list(scratch),
        compiler_params=pltpu.CompilerParams(vmem_limit_bytes=56 * 1024 * 1024),
        cost_estimate=pl.CostEstimate(flops=flops, bytes_accessed=4_000_000, transcendentals=0),
    )


def shifted(x, axis, distance):
    count = lax.axis_size(axis)
    return lax.ppermute(x, axis, [(i, (i + distance) % count) for i in range(count)])


def shards(face_matrix, couple_x, couple_y, skeleton, redundant):
    a, cx, cy = face_matrix[0], couple_x[0], couple_y[0]
    perm = jnp.concatenate([skeleton[0], redundant[0]], axis=-1)[:, None, :]
    square = jax.ShapeDtypeStruct((NF, F, F), f32)
    cxt, cyt, gx, gy = call(first_kernel, (square,) * 4)(cx, cy)
    gx_in = shifted(gx, "gx", 1)
    gy_in = shifted(gy[NF - 1 :], "gy", 1)
    k_local = call(local_kernel, square)(cx, cy, gy)
    v, px, py, sk = call(
        main_kernel,
        (
            jax.ShapeDtypeStruct((NF, R, F), f32),
            square,
            square,
            jax.ShapeDtypeStruct((NF, S, S), f32),
        ),
        [pltpu.VMEM((NF, F, F), bf16), pltpu.VMEM((NF, F, F), f32), pltpu.VMEM((8, 128), f32)],
    )(a, k_local, gx_in, gy_in, perm, cxt, cyt)
    px_in = shifted(px, "gx", 1)
    vx_in = shifted(v, "gx", -1)
    py_in = shifted(py[NF - 1 :], "gy", 1)
    vy_in = shifted(v[:1], "gy", -1)
    part = call(own_kernel, square)(a, cy, v, py)
    out = call(last_kernel, square)(part, cx, cy[NF - 1 :], vx_in, vy_in, px_in, py_in)
    return out[None], sk[None]


def solution(mesh):
    spec4 = P("gx", "gy", None, None)
    spec3 = P("gx", "gy", None)
    return jax.shard_map(
        shards,
        mesh=mesh,
        in_specs=(spec4, spec4, spec4, spec3, spec3),
        out_specs=(spec4, spec4),
        check_vma=False,
    )
```

```python
import functools

import jax
import jax.numpy as jnp
from jax import lax
from jax.experimental import pallas as pl
from jax.experimental.pallas import tpu as pltpu
from jax.sharding import PartitionSpec as P

F = 256
S = 96
R = 160
B = 32
NF = 4
PACK = 240
HALF = 136
GROUPS = ((0, 4),)
f32 = jnp.float32
bf16 = jnp.bfloat16
HI = lax.Precision.HIGHEST
NN = (((1,), (0,)), ((), ()))
NT = (((1,), (1,)), ((), ()))


def nn(a, b):
    return lax.dot_general(a, b, NN, precision=HI, preferred_element_type=f32)


def nt(a, b):
    return lax.dot_general(a, b, NT, precision=HI, preferred_element_type=f32)


def split3(x):
    hi = x.astype(bf16)
    rest = x - hi.astype(f32)
    mid = rest.astype(bf16)
    low = (rest - mid.astype(f32)).astype(bf16)
    return hi, mid, low


def choose(q, x, dims=NN):
    hi, mid, low = split3(x)
    dot = functools.partial(lax.dot_general, dimension_numbers=dims, preferred_element_type=f32)
    return (dot(q, hi) + dot(q, mid)) + dot(q, low)


def choose_columns(x, q):
    hi, mid, low = split3(x)
    dot = functools.partial(lax.dot_general, dimension_numbers=NT, preferred_element_type=f32)
    return (dot(hi, q) + dot(mid, q)) + dot(low, q)


def onehot(perm):
    wide = jnp.broadcast_to(perm, (128, F))
    column = jnp.concatenate([wide[:, :128].T, wide[:, 128:].T], axis=0)
    column = jnp.concatenate([column, column], axis=1)
    point = lax.broadcasted_iota(jnp.int32, (F, F), 1).astype(f32)
    return jnp.where(column == point, 1.0, 0.0).astype(bf16)


def inverse_factor(d):
    lane = lax.broadcasted_iota(jnp.int32, (8, 128), 1)
    sub = lax.broadcasted_iota(jnp.int32, (8, 128), 0)
    base = lane - lax.rem(lane, B)
    inner = lane - base
    dv = [d[8 * v : 8 * v + 8] for v in range(4)]
    ev = [jnp.where(inner == sub + 8 * v, 1.0, 0.0).astype(f32) for v in range(4)]

    def row(x, j):
        return jnp.broadcast_to(x[j : j + 1, :], (8, 128))

    out = []
    for s in range(4):
        cols = {}
        for j in range(8):
            index = base + (8 * s + j)
            for v in range(s, 4):
                cols[j, v] = jnp.take_along_axis(dv[v], index, axis=1)
        scale = jnp.ones((8, 128), f32)
        for j in range(8):
            pivot = row(cols[j, s], j)
            recip = 1.0 / pivot
            row_d = row(dv[s], j)
            row_e = row(ev[s], j)
            heads = {jj: row(cols[j, s], jj) for jj in range(j + 1, 8)}
            for v in range(s, 4):
                mult = cols[j, v] * recip
                if v == s:
                    mult = jnp.where(sub > j, mult, 0.0)
                for jj in range(j + 1, 8):
                    cols[jj, v] = cols[jj, v] - mult * heads[jj]
                dv[v] = dv[v] - mult * row_d
                ev[v] = ev[v] - mult * row_e
            scale = jnp.where(sub == j, pivot, scale)
        root = lax.rsqrt(scale)
        root = root * (1.5 - 0.5 * scale * root * root)
        out.append(ev[s] * root)
    return jnp.concatenate(out, axis=0)


def spread(x, offset, n):
    lane = lax.broadcasted_iota(jnp.int32, (B, 128), 1)
    rows = []
    for g in range(n):
        piece = x[B * g : B * g + B]
        shift = (B * g - offset) % 128
        if shift:
            piece = pltpu.roll(piece, shift, 1)
        rows.append(jnp.where((lane >= B * g) & (lane < B * g + B), piece, 0.0))
    return rows


def eliminate(blocks, first, n):
    lane = lax.broadcasted_iota(jnp.int32, (B, 128), 1)
    wide = blocks[0].shape
    wide_lane = lax.broadcasted_iota(jnp.int32, wide, 1)
    wide_row = lax.rem(lax.broadcasted_iota(jnp.int32, wide, 0), B)
    count = len(blocks)
    blocks = list(blocks)
    out = []
    for k in range(count):
        at = first + B * k
        tile = slice(at // 128 * 128, at // 128 * 128 + 128)
        diag = spread(blocks[k][:, tile], at % 128, n)
        inv = inverse_factor(functools.reduce(jnp.add, diag))
        inv_bd = jnp.concatenate(
            [jnp.where((lane >= B * g) & (lane < B * g + B), inv, 0.0) for g in range(n)], axis=0
        )[:, : B * n]
        inside = (wide_lane >= at) & (wide_lane < at + B)
        if k + 1 < count:
            below = jnp.concatenate(
                [r for i in range(k + 1, count) for r in spread(blocks[i][:, tile], at % 128, n)], axis=0
            )[:, : B * n]
            lower = nt(below, inv_bd)
        top = nn(inv_bd, jnp.where(inside, jnp.where(wide_lane == wide_row + at, 1.0, 0.0), blocks[k]))
        out.append(jnp.where(wide_lane < at + B, top, 0.0))
        if k + 1 < count:
            step = nn(lower, top)
            for i in range(k + 1, count):
                rest = jnp.where(inside, 0.0, blocks[i])
                blocks[i] = rest - step[B * n * (i - k - 1) : B * n * (i - k)]
    return out


def stack(faces, i):
    return jnp.concatenate([x[B * i : B * i + B] for x in faces], axis=0)


def unstack(blocks, g):
    return jnp.concatenate([b[B * g : B * g + B] for b in blocks], axis=0)


def pack_factor(interp_t, z):
    lane = lax.broadcasted_iota(jnp.int32, (R, 128), 1)
    wide = jnp.concatenate([interp_t, jnp.zeros((R, 128 - S), f32)], axis=1)
    first = jnp.where(lane < S, wide, z[:, :128])
    right = z[:, 128:]
    lane = lane[:B]
    mixed = jnp.where(lane < 96, right[96:128], pltpu.roll(right[32:64], 96, 1))
    lane = lane[:16]
    halves = jnp.where(lane < 64, right[64:80], pltpu.roll(right[80:96], 64, 1))
    return jnp.concatenate([first, right[128:160], mixed, halves], axis=0)


def unpack_factor(x):
    lane = lax.broadcasted_iota(jnp.int32, (R, 128), 1)
    left = jnp.where(lane < S, 0.0, x[:R])
    lane = lane[:B]
    mixed = x[192:224]
    one = jnp.where(lane < 32, pltpu.roll(mixed, 32, 1), 0.0)
    three = jnp.where(lane < 96, mixed, 0.0)
    halves = x[224:240]
    two = jnp.concatenate([halves, pltpu.roll(halves, 64, 1)], axis=0)
    two = jnp.where(lane < 64, two, 0.0)
    right = jnp.concatenate([jnp.zeros((B, 128), f32), one, two, three, x[160:192]], axis=0)
    return x[:R, :S], jnp.concatenate([left, right], axis=1)


def pack_symmetric(x):
    row = lax.broadcasted_iota(jnp.int32, (128, 128), 0)
    lane = lax.broadcasted_iota(jnp.int32, (128, 128), 1)
    upper, lower = x[:128, :128], x[128:, 128:]
    both = jnp.where(row >= lane, upper, lower)
    diag = jnp.sum(jnp.where(row == lane, lower, 0.0), axis=0, keepdims=True)
    diag = jnp.broadcast_to(diag, (8, 128))
    main = jnp.concatenate([both, x[:128, 128:]], axis=1)
    return jnp.concatenate([main, jnp.concatenate([diag, diag], axis=1)], axis=0)


def unpack_symmetric(x):
    row = lax.broadcasted_iota(jnp.int32, (128, 128), 0)
    lane = lax.broadcasted_iota(jnp.int32, (128, 128), 1)
    both, side = x[:128, :128], x[:128, 128:]
    turned = both.T
    upper = jnp.where(row >= lane, both, turned)
    diag = jnp.broadcast_to(x[128:129, :128], (128, 128))
    lower = jnp.where(row < lane, both, jnp.where(row == lane, diag, turned))
    return jnp.concatenate(
        [jnp.concatenate([upper, side], axis=1), jnp.concatenate([side.T, lower], axis=1)], axis=0
    )


def update(near, interp_t, z):
    rest = near[S:] - nn(interp_t, near[:S])
    p = nn(z, jnp.concatenate([near[:S], rest], axis=0))
    pt = p.T
    return nt(pt, pt)


def own_kernel(perm, cx, cy, ex, ey, k_out):
    for f in range(NF):
        q = onehot(perm[f])
        x = choose(q, cx[f])
        ex[f] = x
        y = choose(q, cy[f])
        ey[f] = y
        k_out[f] = nt(x[:S], x) + nt(y[:S], y)


def next_kernel(perm_x, perm_y, cx, cy, after, dx, dy, gx, gy):
    for f in range(NF):
        x = choose(onehot(perm_x[f]), cx[f], NT)
        dx[f] = x
        gx[f] = nt(x[:S], x)
    y = choose(onehot(perm_y[0]), cy[NF - 1], NT)
    dy[0] = y
    gy[0] = nt(y[:S], y)


def rest_kernel(perm, a, cy, k_own, dy_last, ap, dy, k_out):
    for f in range(NF):
        q = onehot(perm[f])
        ap[f] = choose(q, choose_columns(a[f], q))
        if f:
            y = choose(q, cy[f - 1], NT)
            dy[f - 1] = y
            k_out[f] = k_own[f] + nt(y[:S], y)
        else:
            k_out[f] = k_own[f]
    dy[NF - 1] = dy_last[0]


def main_kernel(lo, n, k_ref, gx, gy, ap, ex, ey, factor_out, plus_x, plus_y, sk_out):
    grams = []
    tails = []
    for f in range(n):
        k = k_ref[lo + f] + gx[lo + f]
        if lo + f == 0:
            k = k + gy[0]
        grams.append(k[:, :128])
        tails.append(k[:, 128:].T)
    done = eliminate([stack(grams, i) for i in range(S // B)], 0, n)
    systems = []
    interps = []
    for f in range(n):
        inv = unstack(done, f)[:, :S]
        rows = jnp.concatenate([grams[f].T[S:, :S], tails[f]], axis=0)
        jr = nn(nt(rows, inv), inv)
        interps.append(jr)
        xr = ap[lo + f, S:, :] - nn(jr, ap[lo + f, :S, :])
        t = xr[:, :S]
        systems.append(jnp.concatenate([t, xr[:, S:] - nt(t, jr)], axis=1))
    done = eliminate([stack(systems, i) for i in range(R // B)], S, n)
    for f in range(n):
        z = unstack(done, f)
        factor_out[f] = pack_factor(interps[f], z)
        tall_lane = lax.broadcasted_iota(jnp.int32, (R, F), 1)
        z0 = jnp.where(tall_lane < S, 0.0, z)
        st = z[:, :128].T[:S]
        sk_out[f] = ap[lo + f, :S, :S] - nt(st, st)
        plus_x[f] = pack_symmetric(update(ex[lo + f], interps[f], z0))
        if lo + f == NF - 1:
            plus_y[0] = pack_symmetric(update(ey[lo + f], interps[f], z0))


def inner_kernel(a, dy, ey, *refs):
    factors, out = refs[:-1], refs[-1]
    where = [(g, f) for g, (lo, hi) in enumerate(GROUPS) for f in range(hi - lo)]
    for f in range(NF):
        x = a[f]
        if f:
            g, at = where[f - 1]
            x = x - update(ey[f - 1], *unpack_factor(factors[g][at]))
        if f + 1 < NF:
            g, at = where[f + 1]
            x = x - update(dy[f], *unpack_factor(factors[g][at]))
        out[f] = x


def last_kernel(part, dx, dy, factor_y, plus_y, *refs):
    count = len(GROUPS)
    factors, pluses, out = refs[:count], refs[count : 2 * count], refs[-1]
    where = [(g, f) for g, (lo, hi) in enumerate(GROUPS) for f in range(hi - lo)]
    for f in range(NF):
        g, at = where[f]
        x = part[f] - update(dx[f], *unpack_factor(factors[g][at]))
        packed = pluses[g][at]
        if f == 0:
            packed = packed + plus_y[0]
        if f + 1 == NF:
            x = x - update(dy[NF - 1], *unpack_factor(factor_y[0]))
        out[f] = x - unpack_symmetric(packed)


def call(body, outs, in_specs=None):
    extra = {} if in_specs is None else {"in_specs": in_specs}
    return pl.pallas_call(
        body,
        out_shape=outs,
        **extra,
        compiler_params=pltpu.CompilerParams(vmem_limit_bytes=24 * 1024 * 1024),
        cost_estimate=pl.CostEstimate(flops=1_000_000_000, bytes_accessed=4_000_000, transcendentals=0),
    )


def arr(*shape):
    return jax.ShapeDtypeStruct(shape, f32)


def shifted(x, axis, distance):
    count = lax.axis_size(axis)
    return lax.ppermute(x, axis, [(i, (i + distance) % count) for i in range(count)])


def shards(face_matrix, couple_x, couple_y, skeleton, redundant):
    a, cx, cy = face_matrix[0], couple_x[0], couple_y[0]
    perm = jnp.concatenate([skeleton[0], redundant[0]], axis=-1).astype(f32)[:, None, :]
    perm_x = shifted(perm, "gx", -1)
    perm_y = shifted(perm[:1], "gy", -1)
    square = arr(NF, F, F)
    ex, ey, k_own = call(own_kernel, (square, square, arr(NF, S, F)))(perm, cx, cy)
    whole = pl.BlockSpec(memory_space=pltpu.VMEM)
    dx, dy_last, gx, gy = call(
        next_kernel,
        (square, arr(1, F, F), arr(NF, S, F), arr(1, S, F)),
        [whole] * 4 + [pl.BlockSpec(memory_space=pl.ANY)],
    )(perm_x, perm_y, cx, cy, k_own)
    gx_in = shifted(gx, "gx", 1)
    gy_in = shifted(gy, "gy", 1)
    ap, dy, k_loc = call(rest_kernel, (square, square, arr(NF, S, F)))(perm, a, cy, k_own, dy_last)
    factors, blocks, factors_in, plus_in = [], [], [], []
    for lo, hi in GROUPS:
        n = hi - lo
        factor, plus_x, plus_y, sk = call(
            functools.partial(main_kernel, lo, n),
            (arr(n, PACK, 128), arr(n, HALF, F), arr(1, HALF, F), arr(n, S, S)),
        )(k_loc, gx_in, gy_in, ap, ex, ey)
        factors.append(factor)
        blocks.append(sk)
        factors_in.append(shifted(factor, "gx", -1))
        plus_in.append(shifted(plus_x, "gx", 1))
        if lo == 0:
            factor_y = shifted(factor[:1], "gy", -1)
        if hi == NF:
            plus_y_in = shifted(plus_y, "gy", 1)
    part = call(inner_kernel, square)(a, dy, ey, *factors)
    out = call(last_kernel, square)(part, dx, dy, factor_y, plus_y_in, *factors_in, *plus_in)
    sk = blocks[0] if len(blocks) == 1 else jnp.concatenate(blocks, axis=0)
    return out[None], sk[None]


def solution(mesh):
    spec4 = P("gx", "gy", None, None)
    spec3 = P("gx", "gy", None)
    return jax.shard_map(
        shards,
        mesh=mesh,
        in_specs=(spec4, spec4, spec4, spec3, spec3),
        out_specs=(spec4, spec4),
        check_vma=False,
    )
```

```python
import functools

import jax
import jax.numpy as jnp
from jax import lax
from jax.experimental import pallas as pl
from jax.experimental.pallas import tpu as pltpu
from jax.sharding import PartitionSpec as P

F = 256
S = 96
R = 160
B = 32
NF = 4
MINUS = 5000000000
HALF = 136
f32 = jnp.float32
bf16 = jnp.bfloat16
HI = lax.Precision.HIGHEST
NN = (((1,), (0,)), ((), ()))
NT = (((1,), (1,)), ((), ()))


def nn(a, b):
    return lax.dot_general(a, b, NN, precision=HI, preferred_element_type=f32)


def nt(a, b):
    return lax.dot_general(a, b, NT, precision=HI, preferred_element_type=f32)


def split2(x):
    hi = x.astype(bf16)
    return hi, (x - hi.astype(f32)).astype(bf16)


def near32(a, b, dims):
    ah, al = split2(a)
    bh, bl = split2(b) if b is not a else (ah, al)
    dot = functools.partial(lax.dot_general, dimension_numbers=dims, preferred_element_type=f32)
    return dot(ah, bh) + (dot(ah, bl) + dot(al, bh))


def nn3(a, b):
    return near32(a, b, NN)


def nt3(a, b):
    return near32(a, b, NT)


def split3(x):
    hi = x.astype(bf16)
    rest = x - hi.astype(f32)
    mid = rest.astype(bf16)
    low = (rest - mid.astype(f32)).astype(bf16)
    return hi, mid, low


def choose(q, pieces, dims=NN):
    hi, mid, low = pieces
    dot = functools.partial(lax.dot_general, dimension_numbers=dims, preferred_element_type=f32)
    return (dot(q, hi) + dot(q, mid)) + dot(q, low)


def choose_columns(x, q):
    hi, mid, low = split3(x)
    dot = functools.partial(lax.dot_general, dimension_numbers=NT, preferred_element_type=f32)
    return (dot(hi, q) + dot(mid, q)) + dot(low, q)


def onehot(skel):
    point = lax.broadcasted_iota(jnp.int32, (F, S), 0)
    hit = jnp.where(point == skel, 1.0, 0.0).astype(bf16)
    chosen = lax.dot_general(jnp.ones((16, S), bf16), hit, NT, preferred_element_type=f32)
    row = lax.broadcasted_iota(jnp.int32, (F, F), 0)
    lane = lax.broadcasted_iota(jnp.int32, (F, F), 1)
    upto = jnp.where(row <= lane, 1.0, 0.0).astype(bf16)
    count = lax.dot_general(chosen.astype(bf16), upto, NN, preferred_element_type=f32)
    own = lax.broadcasted_iota(jnp.int32, (16, F), 1).astype(f32)
    place = jnp.where(chosen > 0.5, count - 1.0, own - count + float(S))
    return jnp.where(jnp.broadcast_to(place[:1], (F, F)) == row.astype(f32), 1.0, 0.0).astype(bf16)


def inverse_factor(d):
    lane = lax.broadcasted_iota(jnp.int32, (8, 128), 1)
    sub = lax.broadcasted_iota(jnp.int32, (8, 128), 0)
    base = lane - lax.rem(lane, B)
    inner = lane - base
    dv = [d[8 * v : 8 * v + 8] for v in range(4)]
    ev = [jnp.where(inner == sub + 8 * v, 1.0, 0.0).astype(f32) for v in range(4)]

    def row(x, j):
        return jnp.broadcast_to(x[j : j + 1, :], (8, 128))

    out = []
    for s in range(4):
        cols = {}
        for j in range(8):
            index = base + (8 * s + j)
            for v in range(s, 4):
                cols[j, v] = jnp.take_along_axis(dv[v], index, axis=1)
        scale = jnp.ones((8, 128), f32)
        for j in range(8):
            pivot = row(cols[j, s], j)
            recip = 1.0 / pivot
            row_d = row(dv[s], j)
            row_e = row(ev[s], j)
            heads = {jj: row(cols[j, s], jj) for jj in range(j + 1, 8)}
            for v in range(s, 4):
                mult = cols[j, v] * recip
                if v == s:
                    mult = jnp.where(sub > j, mult, 0.0)
                for jj in range(j + 1, 8):
                    cols[jj, v] = cols[jj, v] - mult * heads[jj]
                dv[v] = dv[v] - mult * row_d
                ev[v] = ev[v] - mult * row_e
            scale = jnp.where(sub == j, pivot, scale)
        root = lax.rsqrt(scale)
        root = root * (1.5 - 0.5 * scale * root * root)
        out.append(ev[s] * root)
    return jnp.concatenate(out, axis=0)


def spread(x, offset, n):
    lane = lax.broadcasted_iota(jnp.int32, (B, 128), 1)
    rows = []
    for g in range(n):
        piece = x[B * g : B * g + B]
        shift = (B * g - offset) % 128
        if shift:
            piece = pltpu.roll(piece, shift, 1)
        rows.append(jnp.where((lane >= B * g) & (lane < B * g + B), piece, 0.0))
    return rows


def eliminate(blocks, first, n, dot_nn, dot_nt):
    lane = lax.broadcasted_iota(jnp.int32, (B, 128), 1)
    wide = blocks[0].shape
    wide_lane = lax.broadcasted_iota(jnp.int32, wide, 1)
    wide_row = lax.rem(lax.broadcasted_iota(jnp.int32, wide, 0), B)
    count = len(blocks)
    blocks = list(blocks)
    out = []
    for k in range(count):
        at = first + B * k
        tile = slice(at // 128 * 128, at // 128 * 128 + 128)
        diag = spread(blocks[k][:, tile], at % 128, n)
        inv = inverse_factor(functools.reduce(jnp.add, diag))
        inv_bd = jnp.concatenate(
            [jnp.where((lane >= B * g) & (lane < B * g + B), inv, 0.0) for g in range(n)], axis=0
        )[:, : B * n]
        inside = (wide_lane >= at) & (wide_lane < at + B)
        if k + 1 < count:
            below = [
                jnp.concatenate(spread(blocks[i][:, tile], at % 128, n), axis=0)[:, : B * n]
                for i in range(k + 1, count)
            ]
        top = dot_nn(inv_bd, jnp.where(inside, jnp.where(wide_lane == wide_row + at, 1.0, 0.0), blocks[k]))
        out.append(jnp.where(wide_lane < at + B, top, 0.0))
        if k + 1 < count:
            lower = dot_nt(below[0], inv_bd)
            blocks[k + 1] = jnp.where(inside, 0.0, blocks[k + 1]) - dot_nn(lower, top)
        if k + 2 < count:
            lower = dot_nt(jnp.concatenate(below[1:], axis=0), inv_bd)
            step = dot_nn(lower, top)
            for i in range(k + 2, count):
                rest = jnp.where(inside, 0.0, blocks[i])
                blocks[i] = rest - step[B * n * (i - k - 2) : B * n * (i - k - 1)]
    return out


def stack(faces, i):
    return jnp.concatenate([x[B * i : B * i + B] for x in faces], axis=0)


def unstack(blocks, g):
    return jnp.concatenate([b[B * g : B * g + B] for b in blocks], axis=0)


def lanes(rows):
    return lax.broadcasted_iota(jnp.int32, (rows, 128), 1)


def pack_interp(interp_t):
    wide = jnp.concatenate([interp_t, jnp.zeros((R, 128 - S), f32)], axis=1)
    tail = wide[120:]
    side = jnp.concatenate([pltpu.roll(tail, 96, 1), pltpu.roll(tail, 64, 1), pltpu.roll(tail, 32, 1)], axis=0)
    return jnp.where(lanes(120) < S, wide[:120], side)


def unpack_interp(x):
    lane = lanes(40)
    tail = jnp.where(
        lane < 32,
        pltpu.roll(x[:40], 32, 1),
        jnp.where(lane < 64, pltpu.roll(x[40:80], 64, 1), pltpu.roll(x[80:120], 96, 1)),
    )
    return jnp.concatenate([x, tail], axis=0)[:, :S]


def pack_inverse(z):
    left, right = z[:, :128], z[:, 128:]
    lane = lanes(B)
    mixed = jnp.where(lane < 96, right[96:128], pltpu.roll(right[32:64], 96, 1))
    halves = jnp.where(lanes(16) < 64, right[64:80], pltpu.roll(right[80:96], 64, 1))
    lane = lanes(40)
    column = left[120:]
    for q in (2, 1, 0):
        column = jnp.where(lane < 32 * (q + 1), pltpu.roll(left[40 * q : 40 * q + 40], 32 * (q + 1), 1), column)
    return jnp.concatenate([right[128:160], mixed, halves, column], axis=0)


def unpack_inverse(x):
    lane = lanes(B)
    mixed = x[32:64]
    one = jnp.where(lane < 32, pltpu.roll(mixed, 32, 1), 0.0)
    three = jnp.where(lane < 96, mixed, 0.0)
    halves = x[64:80]
    two = jnp.concatenate([halves, pltpu.roll(halves, 64, 1)], axis=0)
    two = jnp.where(lane < 64, two, 0.0)
    right = jnp.concatenate([jnp.zeros((B, 128), f32), one, two, three, x[:32]], axis=0)
    column = x[80:120]
    left = jnp.concatenate([pltpu.roll(column, 96, 1), pltpu.roll(column, 64, 1), pltpu.roll(column, 32, 1), column], axis=0)
    left = jnp.where(lanes(R) < S, 0.0, left)
    return jnp.concatenate([left, right], axis=1)


def pack_symmetric(x):
    row = lax.broadcasted_iota(jnp.int32, (128, 128), 0)
    lane = lax.broadcasted_iota(jnp.int32, (128, 128), 1)
    upper, lower = x[:128, :128], x[128:, 128:]
    both = jnp.where(row >= lane, upper, lower)
    diag = jnp.sum(jnp.where(row == lane, lower, 0.0), axis=0, keepdims=True)
    diag = jnp.broadcast_to(diag, (8, 128))
    main = jnp.concatenate([both, x[:128, 128:]], axis=1)
    return jnp.concatenate([main, jnp.concatenate([diag, diag], axis=1)], axis=0)


def unpack_symmetric(x):
    row = lax.broadcasted_iota(jnp.int32, (128, 128), 0)
    lane = lax.broadcasted_iota(jnp.int32, (128, 128), 1)
    both, side = x[:128, :128], x[:128, 128:]
    turned = both.T
    upper = jnp.where(row >= lane, both, turned)
    diag = jnp.broadcast_to(x[128:129, :128], (128, 128))
    lower = jnp.where(row < lane, both, jnp.where(row == lane, diag, turned))
    return jnp.concatenate(
        [jnp.concatenate([upper, side], axis=1), jnp.concatenate([side.T, lower], axis=1)], axis=0
    )


def update(near, interp_t, z):
    rest = near[S:] - nn3(interp_t, near[:S])
    p = nn3(z, jnp.concatenate([near[:S], rest], axis=0))
    pt = p.T
    return nt3(pt, pt)


def split_kernel(cx, cy, xs, ys):
    for f in range(NF):
        for i, piece in enumerate(split3(cx[f])):
            xs[f, i] = piece
        for i, piece in enumerate(split3(cy[f])):
            ys[f, i] = piece


def three(ref, f):
    return ref[f, 0], ref[f, 1], ref[f, 2]


def next_kernel(skel_x, skel_y, xs, ys, dx, gx, dy, gy):
    y = choose(onehot(skel_y[:1, :]), three(ys, NF - 1), NT)
    dy[0] = y
    gy[0] = nt(y[:S], y)
    for f in range(NF):
        x = choose(onehot(skel_x[f : f + 1, :]), three(xs, f), NT)
        dx[f] = x
        gx[f] = nt(x[:S], x)


def local_kernel(skel, a, xs, ys, after, ex, ey, ap, dy, k_out):
    for f in range(NF):
        q = onehot(skel[f : f + 1, :])
        x = choose(q, three(xs, f))
        ex[f] = x
        y = choose(q, three(ys, f))
        ey[f] = y
        k = nt(x[:S], x) + nt(y[:S], y)
        if f:
            y = choose(q, three(ys, f - 1), NT)
            dy[f - 1] = y
            k = k + nt(y[:S], y)
        k_out[f] = k
        ap[f] = choose(q, split3(choose_columns(a[f], q)))


def interp_kernel(k_ref, gx, gy, interp_out, packed_out):
    grams = []
    rows = []
    for f in range(NF):
        k = k_ref[f] + gx[f]
        if f == 0:
            k = k + gy[0]
        grams.append(k[:, :128])
        rows.append(jnp.concatenate([k[:, :128].T, k[:, 128:].T], axis=0)[S:])
    done = eliminate([stack(grams, i) for i in range(S // B)], 0, NF, nn, nt)
    for f in range(NF):
        inv = unstack(done, f)[:, :S]
        interp_t = nn(nt(rows[f], inv), inv)
        interp_out[f] = interp_t
        packed_out[f] = pack_interp(interp_t)


def factor_kernel(ap, interp, z_out, packed_out, first_out, sk_out):
    systems = []
    for f in range(NF):
        interp_t = interp[f]
        xr = ap[f, S:, :] - nn3(interp_t, ap[f, :S, :])
        t = xr[:, :S]
        systems.append(jnp.concatenate([t, xr[:, S:] - nt3(t, interp_t)], axis=1))
    done = eliminate([stack(systems, i) for i in range(R // B)], S, NF, nn3, nt3)
    lane = lax.broadcasted_iota(jnp.int32, (R, F), 1)
    for f in range(NF):
        z = unstack(done, f)
        z_out[f] = jnp.where(lane < S, 0.0, z)
        packed = pack_inverse(z)
        packed_out[f] = packed
        if f == 0:
            first_out[0] = jnp.concatenate([packed, pack_interp(interp[0])], axis=0)
        st = z[:, :128].T[:S]
        sk_out[f] = ap[f, :S, :S] - nt3(st, st)


def plus_kernel(ex, ey, interp, z, interp_in, plus_x, plus_y):
    for f in range(NF):
        plus_x[f] = pack_symmetric(update(ex[f], interp[f], z[f]))
    plus_y[0] = pack_symmetric(update(ey[NF - 1], interp[NF - 1], z[NF - 1]))


def inner_kernel(a, ey, dy, interp, z, after, out):
    for f in range(NF):
        x = a[f]
        if f:
            x = x - update(ey[f - 1], interp[f - 1], z[f - 1])
        if f + 1 < NF:
            x = x - update(dy[f], interp[f + 1], z[f + 1])
        out[f] = x


def minus_kernel(part, dx, dy, interp, inverse, both, out):
    for f in range(NF):
        x = part[f] - update(dx[f], unpack_interp(interp[f]), unpack_inverse(inverse[f]))
        if f + 1 == NF:
            y = both[0]
            x = x - update(dy[0], unpack_interp(y[120:]), unpack_inverse(y[:120]))
        out[f] = x


def last_kernel(part, plus_x, plus_y, out):
    for f in range(NF):
        packed = plus_x[f]
        if f == 0:
            packed = packed + plus_y[0]
        out[f] = part[f] - unpack_symmetric(packed)


def call(body, outs, count, unread=(), cost=1000):
    specs = [pl.BlockSpec(memory_space=pl.ANY if i in unread else pltpu.VMEM) for i in range(count)]
    return pl.pallas_call(
        body,
        out_shape=outs,
        in_specs=specs,
        compiler_params=pltpu.CompilerParams(vmem_limit_bytes=20 * 1024 * 1024),
        cost_estimate=pl.CostEstimate(flops=cost, bytes_accessed=1000, transcendentals=0),
    )


def arr(*shape):
    return jax.ShapeDtypeStruct(shape, f32)


def shifted(x, axis, distance):
    count = lax.axis_size(axis)
    return lax.ppermute(x, axis, [(i, (i + distance) % count) for i in range(count)])


def shards(face_matrix, couple_x, couple_y, skeleton, redundant):
    a, cx, cy, skel = face_matrix[0], couple_x[0], couple_y[0], skeleton[0]
    skel_x = shifted(skel, "gx", -1)
    skel_y = shifted(skel, "gy", -1)
    square = arr(NF, F, F)
    pieces = jax.ShapeDtypeStruct((NF, 3, F, F), bf16)
    xs, ys = call(split_kernel, (pieces, pieces), 2)(cx, cy)
    dx, gx, dy_last, gy = call(next_kernel, (square, arr(NF, S, F), arr(1, F, F), arr(1, S, F)), 4)(
        skel_x, skel_y, xs, ys
    )
    gx_in = shifted(gx, "gx", 1)
    gy_in = shifted(gy, "gy", 1)
    ex, ey, ap, dy, k_loc = call(
        local_kernel, (square, square, square, arr(NF - 1, F, F), arr(NF, S, F)), 5, (4,)
    )(skel, a, xs, ys, gy)
    interp, interp_packed = call(interp_kernel, (arr(NF, R, S), arr(NF, 120, 128)), 3)(k_loc, gx_in, gy_in)
    interp_in = shifted(interp_packed, "gx", -1)
    z, z_packed, z_first, sk = call(
        factor_kernel, (arr(NF, R, F), arr(NF, 120, 128), arr(1, 240, 128), arr(NF, S, S)), 2
    )(ap, interp)
    z_in = shifted(z_packed, "gx", -1)
    first_in = shifted(z_first, "gy", -1)
    plus_x, plus_y = call(plus_kernel, (arr(NF, HALF, F), arr(1, HALF, F)), 5, (4,))(ex, ey, interp, z, interp_in)
    plus_x_in = shifted(plus_x, "gx", 1)
    plus_y_in = shifted(plus_y, "gy", 1)
    part = call(inner_kernel, square, 6, (5,))(a, ey, dy, interp, z, plus_y)
    part = call(minus_kernel, square, 6, cost=MINUS)(part, dx, dy_last, interp_in, z_in, first_in)
    out = call(last_kernel, square, 3)(part, plus_x_in, plus_y_in)
    return out[None], sk[None]


def solution(mesh):
    spec4 = P("gx", "gy", None, None)
    spec3 = P("gx", "gy", None)
    return jax.shard_map(
        shards,
        mesh=mesh,
        in_specs=(spec4, spec4, spec4, spec3, spec3),
        out_specs=(spec4, spec4),
        check_vma=False,
    )
```

```python
import functools

import jax
import jax.numpy as jnp
from jax import lax
from jax.experimental import pallas as pl
from jax.experimental.pallas import tpu as pltpu
from jax.sharding import PartitionSpec as P

F = 256
S = 96
R = 160
B = 32
NF = 4
MINUS = 5000000000
f32 = jnp.float32
bf16 = jnp.bfloat16
HI = lax.Precision.HIGHEST
NN = (((1,), (0,)), ((), ()))
NT = (((1,), (1,)), ((), ()))


def nn(a, b):
    return lax.dot_general(a, b, NN, precision=HI, preferred_element_type=f32)


def nt(a, b):
    return lax.dot_general(a, b, NT, precision=HI, preferred_element_type=f32)


def split2(x):
    hi = x.astype(bf16)
    return hi, (x - hi.astype(f32)).astype(bf16)


def near32(a, b, dims):
    ah, al = split2(a)
    bh, bl = split2(b) if b is not a else (ah, al)
    dot = functools.partial(lax.dot_general, dimension_numbers=dims, preferred_element_type=f32)
    return dot(ah, bh) + (dot(ah, bl) + dot(al, bh))


def nn3(a, b):
    return near32(a, b, NN)


def nt3(a, b):
    return near32(a, b, NT)


def split3(x):
    hi = x.astype(bf16)
    rest = x - hi.astype(f32)
    mid = rest.astype(bf16)
    low = (rest - mid.astype(f32)).astype(bf16)
    return hi, mid, low


def choose(q, pieces, dims=NN):
    hi, mid, low = pieces
    dot = functools.partial(lax.dot_general, dimension_numbers=dims, preferred_element_type=f32)
    return (dot(q, hi) + dot(q, mid)) + dot(q, low)


def choose_columns(x, q):
    hi, mid, low = split3(x)
    dot = functools.partial(lax.dot_general, dimension_numbers=NT, preferred_element_type=f32)
    return (dot(hi, q) + dot(mid, q)) + dot(low, q)


def onehot(skel):
    point = lax.broadcasted_iota(jnp.int32, (F, S), 0)
    hit = jnp.where(point == skel, 1.0, 0.0).astype(bf16)
    chosen = lax.dot_general(jnp.ones((16, S), bf16), hit, NT, preferred_element_type=f32)
    row = lax.broadcasted_iota(jnp.int32, (F, F), 0)
    lane = lax.broadcasted_iota(jnp.int32, (F, F), 1)
    upto = jnp.where(row <= lane, 1.0, 0.0).astype(bf16)
    count = lax.dot_general(chosen.astype(bf16), upto, NN, preferred_element_type=f32)
    own = lax.broadcasted_iota(jnp.int32, (16, F), 1).astype(f32)
    place = jnp.where(chosen > 0.5, count - 1.0, own - count + float(S))
    return jnp.where(jnp.broadcast_to(place[:1], (F, F)) == row.astype(f32), 1.0, 0.0).astype(bf16)


def inverse_factor(d):
    lane = lax.broadcasted_iota(jnp.int32, (8, 128), 1)
    sub = lax.broadcasted_iota(jnp.int32, (8, 128), 0)
    base = lane - lax.rem(lane, B)
    inner = lane - base
    dv = [d[8 * v : 8 * v + 8] for v in range(4)]
    ev = [jnp.where(inner == sub + 8 * v, 1.0, 0.0).astype(f32) for v in range(4)]

    def row(x, j):
        return jnp.broadcast_to(x[j : j + 1, :], (8, 128))

    def gather(s):
        found = {}
        for j in range(8):
            index = base + (8 * s + j)
            for v in range(s, 4):
                found[j, v] = jnp.take_along_axis(dv[v], index, axis=1)
        return found

    out = []
    cols = gather(0)
    for s in range(4):
        ahead = gather(s + 1) if s < 3 else {}
        scale = jnp.ones((8, 128), f32)
        for j in range(8):
            pivot = row(cols[j, s], j)
            recip = 1.0 / pivot
            heads = {jj: row(cols[j, s], jj) for jj in range(j + 1, 8)}
            mults = {v: cols[j, v] * recip for v in range(s, 4)}
            mults[s] = jnp.where(sub > j, mults[s], 0.0)
            for v in range(s, 4):
                for jj in range(j + 1, 8):
                    cols[jj, v] = cols[jj, v] - mults[v] * heads[jj]
            if s < 3:
                for jj in range(8):
                    head = row(cols[j, s + 1], jj)
                    for v in range(s + 1, 4):
                        ahead[jj, v] = ahead[jj, v] - mults[v] * head
            row_d = row(dv[s], j)
            row_e = row(ev[s], j)
            for v in range(s, 4):
                dv[v] = dv[v] - mults[v] * row_d
                ev[v] = ev[v] - mults[v] * row_e
            scale = jnp.where(sub == j, pivot, scale)
        root = lax.rsqrt(scale)
        root = root * (1.5 - 0.5 * scale * root * root)
        out.append(ev[s] * root)
        cols = ahead
    return jnp.concatenate(out, axis=0)


def spread(x, offset, n):
    lane = lax.broadcasted_iota(jnp.int32, (B, 128), 1)
    rows = []
    for g in range(n):
        piece = x[B * g : B * g + B]
        shift = (B * g - offset) % 128
        if shift:
            piece = pltpu.roll(piece, shift, 1)
        rows.append(jnp.where((lane >= B * g) & (lane < B * g + B), piece, 0.0))
    return rows


def eliminate(blocks, first, n, dot_nn, dot_nt):
    lane = lax.broadcasted_iota(jnp.int32, (B, 128), 1)
    wide = blocks[0].shape
    wide_lane = lax.broadcasted_iota(jnp.int32, wide, 1)
    wide_row = lax.rem(lax.broadcasted_iota(jnp.int32, wide, 0), B)
    count = len(blocks)
    blocks = list(blocks)
    out = []
    for k in range(count):
        at = first + B * k
        tile = slice(at // 128 * 128, at // 128 * 128 + 128)
        diag = spread(blocks[k][:, tile], at % 128, n)
        inv = inverse_factor(functools.reduce(jnp.add, diag))
        inv_bd = jnp.concatenate(
            [jnp.where((lane >= B * g) & (lane < B * g + B), inv, 0.0) for g in range(n)], axis=0
        )[:, : B * n]
        inside = (wide_lane >= at) & (wide_lane < at + B)
        if k + 1 < count:
            below = [
                jnp.concatenate(spread(blocks[i][:, tile], at % 128, n), axis=0)[:, : B * n]
                for i in range(k + 1, count)
            ]
        top = dot_nn(inv_bd, jnp.where(inside, jnp.where(wide_lane == wide_row + at, 1.0, 0.0), blocks[k]))
        out.append(jnp.where(wide_lane < at + B, top, 0.0))
        if k + 1 < count:
            lower = dot_nt(below[0], inv_bd)
            blocks[k + 1] = jnp.where(inside, 0.0, blocks[k + 1]) - dot_nn(lower, top)
        if k + 2 < count:
            lower = dot_nt(jnp.concatenate(below[1:], axis=0), inv_bd)
            step = dot_nn(lower, top)
            for i in range(k + 2, count):
                rest = jnp.where(inside, 0.0, blocks[i])
                blocks[i] = rest - step[B * n * (i - k - 2) : B * n * (i - k - 1)]
    return out


def stack(faces, i):
    return jnp.concatenate([x[B * i : B * i + B] for x in faces], axis=0)


def unstack(blocks, g):
    return jnp.concatenate([b[B * g : B * g + B] for b in blocks], axis=0)


def lanes(rows):
    return lax.broadcasted_iota(jnp.int32, (rows, 128), 1)


def pack_interp(interp_t):
    wide = jnp.concatenate([interp_t, jnp.zeros((R, 128 - S), f32)], axis=1)
    tail = wide[120:]
    side = jnp.concatenate([pltpu.roll(tail, 96, 1), pltpu.roll(tail, 64, 1), pltpu.roll(tail, 32, 1)], axis=0)
    return jnp.where(lanes(120) < S, wide[:120], side)


def unpack_interp(x):
    lane = lanes(40)
    tail = jnp.where(
        lane < 32,
        pltpu.roll(x[:40], 32, 1),
        jnp.where(lane < 64, pltpu.roll(x[40:80], 64, 1), pltpu.roll(x[80:120], 96, 1)),
    )
    return jnp.concatenate([x, tail], axis=0)[:, :S]


def pack_inverse(z):
    left, right = z[:, :128], z[:, 128:]
    lane = lanes(B)
    mixed = jnp.where(lane < 96, right[96:128], pltpu.roll(right[32:64], 96, 1))
    halves = jnp.where(lanes(16) < 64, right[64:80], pltpu.roll(right[80:96], 64, 1))
    lane = lanes(40)
    column = left[120:]
    for q in (2, 1, 0):
        column = jnp.where(lane < 32 * (q + 1), pltpu.roll(left[40 * q : 40 * q + 40], 32 * (q + 1), 1), column)
    return jnp.concatenate([right[128:160], mixed, halves, column], axis=0)


def unpack_inverse(x):
    lane = lanes(B)
    mixed = x[32:64]
    one = jnp.where(lane < 32, pltpu.roll(mixed, 32, 1), 0.0)
    three = jnp.where(lane < 96, mixed, 0.0)
    halves = x[64:80]
    two = jnp.concatenate([halves, pltpu.roll(halves, 64, 1)], axis=0)
    two = jnp.where(lane < 64, two, 0.0)
    right = jnp.concatenate([jnp.zeros((B, 128), f32), one, two, three, x[:32]], axis=0)
    column = x[80:120]
    left = jnp.concatenate([pltpu.roll(column, 96, 1), pltpu.roll(column, 64, 1), pltpu.roll(column, 32, 1), column], axis=0)
    left = jnp.where(lanes(R) < S, 0.0, left)
    return jnp.concatenate([left, right], axis=1)


def pack_symmetric(x, f=0):
    row = lax.broadcasted_iota(jnp.int32, (128, 128), 0)
    lane = lax.broadcasted_iota(jnp.int32, (128, 128), 1)
    upper, lower = x[:128, :128], x[128:, 128:]
    both = jnp.where(row >= lane, upper, lower)
    diag = jnp.sum(jnp.where(row == lane, lower, 0.0), axis=0, keepdims=True)
    diag = jnp.where(row[:8] == f, jnp.broadcast_to(diag, (8, 128)), 0.0)
    return jnp.concatenate([both, x[:128, 128:]], axis=1), jnp.concatenate([diag, diag], axis=1)


def unpack_symmetric(x, diag):
    row = lax.broadcasted_iota(jnp.int32, (128, 128), 0)
    lane = lax.broadcasted_iota(jnp.int32, (128, 128), 1)
    both, side = x[:, :128], x[:, 128:]
    turned = both.T
    upper = jnp.where(row >= lane, both, turned)
    diag = jnp.broadcast_to(diag[:, :128], (128, 128))
    lower = jnp.where(row < lane, both, jnp.where(row == lane, diag, turned))
    return jnp.concatenate(
        [jnp.concatenate([upper, side], axis=1), jnp.concatenate([side.T, lower], axis=1)], axis=0
    )


def update(near, interp_t, z):
    rest = near[S:] - nn3(interp_t, near[:S])
    p = nn3(z, jnp.concatenate([near[:S], rest], axis=0))
    pt = p.T
    return nt3(pt, pt)


def split_kernel(cx, cy, xs, ys):
    for f in range(NF):
        for i, piece in enumerate(split3(cx[f])):
            xs[f, i] = piece
        for i, piece in enumerate(split3(cy[f])):
            ys[f, i] = piece


def three(ref, f):
    return ref[f, 0], ref[f, 1], ref[f, 2]


def next_kernel(skel_x, skel_y, xs, ys, dx, gx, dy, gy):
    y = choose(onehot(skel_y[:1, :]), three(ys, NF - 1), NT)
    dy[0] = y
    gy[0] = nt(y[:S], y)
    for f in range(NF):
        x = choose(onehot(skel_x[f : f + 1, :]), three(xs, f), NT)
        dx[f] = x
        gx[f] = nt(x[:S], x)


def local_kernel(skel, a, xs, ys, after, ex, ey, ap, dy, k_out):
    for f in range(NF):
        q = onehot(skel[f : f + 1, :])
        x = choose(q, three(xs, f))
        ex[f] = x
        y = choose(q, three(ys, f))
        ey[f] = y
        k = nt(x[:S], x) + nt(y[:S], y)
        if f:
            y = choose(q, three(ys, f - 1), NT)
            dy[f - 1] = y
            k = k + nt(y[:S], y)
        k_out[f] = k
        ap[f] = choose(q, split3(choose_columns(a[f], q)))


def interp_kernel(k_ref, gx, gy, interp_out, packed_out):
    grams = []
    rows = []
    for f in range(NF):
        k = k_ref[f] + gx[f]
        if f == 0:
            k = k + gy[0]
        grams.append(k[:, :128])
        rows.append(jnp.concatenate([k[:, :128].T, k[:, 128:].T], axis=0)[S:])
    done = eliminate([stack(grams, i) for i in range(S // B)], 0, NF, nn, nt)
    for f in range(NF):
        inv = unstack(done, f)[:, :S]
        interp_t = nn(nt(rows[f], inv), inv)
        interp_out[f] = interp_t
        packed_out[f] = pack_interp(interp_t)


def factor_kernel(ap, interp, z_out, packed_out, first_out):
    systems = []
    for f in range(NF):
        interp_t = interp[f]
        xr = ap[f, S:, :] - nn3(interp_t, ap[f, :S, :])
        t = xr[:, :S]
        systems.append(jnp.concatenate([t, xr[:, S:] - nt3(t, interp_t)], axis=1))
    done = eliminate([stack(systems, i) for i in range(R // B)], S, NF, nn3, nt3)
    for f in range(NF):
        z = unstack(done, f)
        z_out[f] = z
        packed = pack_inverse(z)
        packed_out[f] = packed
        if f == 0:
            first_out[0] = jnp.concatenate([packed, pack_interp(interp[0])], axis=0)


def inverse_of(z):
    return jnp.where(lax.broadcasted_iota(jnp.int32, (R, F), 1) < S, 0.0, z)


def plus_kernel(ex, ey, interp, z, interp_in, plus_x, plus_y):
    tail = jnp.zeros((8, F), f32)
    for f in range(NF):
        x, diag = pack_symmetric(update(ex[f], interp[f], inverse_of(z[f])), f)
        plus_x[128 * f : 128 * f + 128, :] = x
        tail = tail + diag
    plus_x[128 * NF :, :] = tail
    x, diag = pack_symmetric(update(ey[NF - 1], interp[NF - 1], inverse_of(z[NF - 1])))
    plus_y[:128, :] = x
    plus_y[128:, :] = diag


def inner_kernel(a, ey, dy, interp, z, ap, after, out, sk_out):
    inverses = [inverse_of(z[f]) for f in range(NF)]
    for f in range(NF):
        x = a[f]
        if f:
            x = x - update(ey[f - 1], interp[f - 1], inverses[f - 1])
        if f + 1 < NF:
            x = x - update(dy[f], interp[f + 1], inverses[f + 1])
        out[f] = x
        st = z[f, :, :128].T[:S]
        sk_out[f] = ap[f, :S, :S] - nt3(st, st)


def minus_kernel(part, dx, dy, interp, inverse, both, out):
    for f in range(NF):
        x = part[f] - update(dx[f], unpack_interp(interp[f]), unpack_inverse(inverse[f]))
        if f + 1 == NF:
            y = both[0]
            x = x - update(dy[0], unpack_interp(y[120:]), unpack_inverse(y[:120]))
        out[f] = x


def last_kernel(part, plus_x, plus_y, out):
    for f in range(NF):
        packed = plus_x[128 * f : 128 * f + 128, :]
        diag = plus_x[128 * NF + f : 128 * NF + f + 1, :]
        if f == 0:
            packed = packed + plus_y[:128, :]
            diag = diag + plus_y[128:129, :]
        out[f] = part[f] - unpack_symmetric(packed, diag)


def call(body, outs, count, unread=(), cost=1000):
    specs = [pl.BlockSpec(memory_space=pl.ANY if i in unread else pltpu.VMEM) for i in range(count)]
    return pl.pallas_call(
        body,
        out_shape=outs,
        in_specs=specs,
        compiler_params=pltpu.CompilerParams(vmem_limit_bytes=20 * 1024 * 1024),
        cost_estimate=pl.CostEstimate(flops=cost, bytes_accessed=1000, transcendentals=0),
    )


def arr(*shape):
    return jax.ShapeDtypeStruct(shape, f32)


def shifted(x, axis, distance):
    count = lax.axis_size(axis)
    return lax.ppermute(x, axis, [(i, (i + distance) % count) for i in range(count)])


def shards(face_matrix, couple_x, couple_y, skeleton, redundant):
    a, cx, cy, skel = face_matrix[0], couple_x[0], couple_y[0], skeleton[0]
    skel_x = shifted(skel, "gx", -1)
    skel_y = shifted(skel, "gy", -1)
    square = arr(NF, F, F)
    pieces = jax.ShapeDtypeStruct((NF, 3, F, F), bf16)
    xs, ys = call(split_kernel, (pieces, pieces), 2)(cx, cy)
    dx, gx, dy_last, gy = call(next_kernel, (square, arr(NF, S, F), arr(1, F, F), arr(1, S, F)), 4)(
        skel_x, skel_y, xs, ys
    )
    gx_in = shifted(gx, "gx", 1)
    gy_in = shifted(gy, "gy", 1)
    ex, ey, ap, dy, k_loc = call(
        local_kernel, (square, square, square, arr(NF - 1, F, F), arr(NF, S, F)), 5, (4,)
    )(skel, a, xs, ys, gy)
    interp, interp_packed = call(interp_kernel, (arr(NF, R, S), arr(NF, 120, 128)), 3)(k_loc, gx_in, gy_in)
    interp_in = shifted(interp_packed, "gx", -1)
    z, z_packed, z_first = call(
        factor_kernel, (arr(NF, R, F), arr(NF, 120, 128), arr(1, 240, 128)), 2
    )(ap, interp)
    z_in = shifted(z_packed, "gx", -1)
    first_in = shifted(z_first, "gy", -1)
    plus_x, plus_y = call(plus_kernel, (arr(128 * NF + 8, F), arr(136, F)), 5, (4,))(ex, ey, interp, z, interp_in)
    plus_x_in = shifted(plus_x, "gx", 1)
    plus_y_in = shifted(plus_y, "gy", 1)
    part, sk = call(inner_kernel, (square, arr(NF, S, S)), 7, (6,))(a, ey, dy, interp, z, ap, plus_y)
    part = call(minus_kernel, square, 6, cost=MINUS)(part, dx, dy_last, interp_in, z_in, first_in)
    out = call(last_kernel, square, 3)(part, plus_x_in, plus_y_in)
    return out[None], sk[None]


def solution(mesh):
    spec4 = P("gx", "gy", None, None)
    spec3 = P("gx", "gy", None)
    return jax.shard_map(
        shards,
        mesh=mesh,
        in_specs=(spec4, spec4, spec4, spec3, spec3),
        out_specs=(spec4, spec4),
        check_vma=False,
    )
```

```python
import functools

import jax
import jax.numpy as jnp
from jax import lax
from jax.experimental import pallas as pl
from jax.experimental.pallas import tpu as pltpu
from jax.sharding import PartitionSpec as P

F = 256
S = 96
R = 160
B = 32
NF = 4
MINUS = 5000000000
f32 = jnp.float32
bf16 = jnp.bfloat16
HI = lax.Precision.HIGHEST
NN = (((1,), (0,)), ((), ()))
NT = (((1,), (1,)), ((), ()))


def nn(a, b):
    return lax.dot_general(a, b, NN, precision=HI, preferred_element_type=f32)


def nt(a, b):
    return lax.dot_general(a, b, NT, precision=HI, preferred_element_type=f32)


def split2(x):
    hi = x.astype(bf16)
    return hi, (x - hi.astype(f32)).astype(bf16)


def near32(a, b, dims):
    ah, al = split2(a)
    bh, bl = split2(b) if b is not a else (ah, al)
    dot = functools.partial(lax.dot_general, dimension_numbers=dims, preferred_element_type=f32)
    return dot(ah, bh) + (dot(ah, bl) + dot(al, bh))


def nn3(a, b):
    return near32(a, b, NN)


def nt3(a, b):
    return near32(a, b, NT)


def split3(x):
    hi = x.astype(bf16)
    rest = x - hi.astype(f32)
    mid = rest.astype(bf16)
    low = (rest - mid.astype(f32)).astype(bf16)
    return hi, mid, low


def choose(q, pieces, dims=NN):
    hi, mid, low = pieces
    dot = functools.partial(lax.dot_general, dimension_numbers=dims, preferred_element_type=f32)
    return (dot(q, hi) + dot(q, mid)) + dot(q, low)


def choose_columns(x, q):
    hi, mid, low = split3(x)
    dot = functools.partial(lax.dot_general, dimension_numbers=NT, preferred_element_type=f32)
    return (dot(hi, q) + dot(mid, q)) + dot(low, q)


def onehot(skel):
    point = lax.broadcasted_iota(jnp.int32, (F, S), 0)
    hit = jnp.where(point == skel, 1.0, 0.0).astype(bf16)
    chosen = lax.dot_general(jnp.ones((16, S), bf16), hit, NT, preferred_element_type=f32)
    row = lax.broadcasted_iota(jnp.int32, (F, F), 0)
    lane = lax.broadcasted_iota(jnp.int32, (F, F), 1)
    upto = jnp.where(row <= lane, 1.0, 0.0).astype(bf16)
    count = lax.dot_general(chosen.astype(bf16), upto, NN, preferred_element_type=f32)
    own = lax.broadcasted_iota(jnp.int32, (16, F), 1).astype(f32)
    place = jnp.where(chosen > 0.5, count - 1.0, own - count + float(S))
    return jnp.where(jnp.broadcast_to(place[:1], (F, F)) == row.astype(f32), 1.0, 0.0).astype(bf16)


def inverse_factor(d):
    lane = lax.broadcasted_iota(jnp.int32, (8, 128), 1)
    sub = lax.broadcasted_iota(jnp.int32, (8, 128), 0)
    base = lane - lax.rem(lane, B)
    inner = lane - base
    dv = [d[8 * v : 8 * v + 8] for v in range(4)]
    ev = [jnp.where(inner == sub + 8 * v, 1.0, 0.0).astype(f32) for v in range(4)]

    def row(x, j):
        return jnp.broadcast_to(x[j : j + 1, :], (8, 128))

    def gather(s):
        found = {}
        for j in range(8):
            index = base + (8 * s + j)
            for v in range(s, 4):
                found[j, v] = jnp.take_along_axis(dv[v], index, axis=1)
        return found

    out = []
    cols = gather(0)
    for s in range(4):
        ahead = gather(s + 1) if s < 3 else {}
        scale = jnp.ones((8, 128), f32)
        for j in range(8):
            pivot = row(cols[j, s], j)
            recip = 1.0 / pivot
            heads = {jj: row(cols[j, s], jj) for jj in range(j + 1, 8)}
            mults = {v: cols[j, v] * recip for v in range(s, 4)}
            mults[s] = jnp.where(sub > j, mults[s], 0.0)
            for v in range(s, 4):
                for jj in range(j + 1, 8):
                    cols[jj, v] = cols[jj, v] - mults[v] * heads[jj]
            if s < 3:
                for jj in range(8):
                    head = row(cols[j, s + 1], jj)
                    for v in range(s + 1, 4):
                        ahead[jj, v] = ahead[jj, v] - mults[v] * head
            row_d = row(dv[s], j)
            row_e = row(ev[s], j)
            for v in range(s, 4):
                dv[v] = dv[v] - mults[v] * row_d
                ev[v] = ev[v] - mults[v] * row_e
            scale = jnp.where(sub == j, pivot, scale)
        root = lax.rsqrt(scale)
        root = root * (1.5 - 0.5 * scale * root * root)
        out.append(ev[s] * root)
        cols = ahead
    return jnp.concatenate(out, axis=0)


def spread(x, offset, n):
    lane = lax.broadcasted_iota(jnp.int32, (B, 128), 1)
    rows = []
    for g in range(n):
        piece = x[B * g : B * g + B]
        shift = (B * g - offset) % 128
        if shift:
            piece = pltpu.roll(piece, shift, 1)
        rows.append(jnp.where((lane >= B * g) & (lane < B * g + B), piece, 0.0))
    return rows


def eliminate(blocks, first, n, dot_nn, dot_nt):
    lane = lax.broadcasted_iota(jnp.int32, (B, 128), 1)
    wide = blocks[0].shape
    wide_lane = lax.broadcasted_iota(jnp.int32, wide, 1)
    wide_row = lax.rem(lax.broadcasted_iota(jnp.int32, wide, 0), B)
    count = len(blocks)
    blocks = list(blocks)
    out = []
    for k in range(count):
        at = first + B * k
        tile = slice(at // 128 * 128, at // 128 * 128 + 128)
        diag = spread(blocks[k][:, tile], at % 128, n)
        inv = inverse_factor(functools.reduce(jnp.add, diag))
        inv_bd = jnp.concatenate(
            [jnp.where((lane >= B * g) & (lane < B * g + B), inv, 0.0) for g in range(n)], axis=0
        )[:, : B * n]
        inside = (wide_lane >= at) & (wide_lane < at + B)
        if k + 1 < count:
            below = [
                jnp.concatenate(spread(blocks[i][:, tile], at % 128, n), axis=0)[:, : B * n]
                for i in range(k + 1, count)
            ]
        top = dot_nn(inv_bd, jnp.where(inside, jnp.where(wide_lane == wide_row + at, 1.0, 0.0), blocks[k]))
        out.append(jnp.where(wide_lane < at + B, top, 0.0))
        if k + 1 < count:
            lower = dot_nt(below[0], inv_bd)
            blocks[k + 1] = jnp.where(inside, 0.0, blocks[k + 1]) - dot_nn(lower, top)
        if k + 2 < count:
            lower = dot_nt(jnp.concatenate(below[1:], axis=0), inv_bd)
            step = dot_nn(lower, top)
            for i in range(k + 2, count):
                rest = jnp.where(inside, 0.0, blocks[i])
                blocks[i] = rest - step[B * n * (i - k - 2) : B * n * (i - k - 1)]
    return out


def stack(faces, i):
    return jnp.concatenate([x[B * i : B * i + B] for x in faces], axis=0)


def unstack(blocks, g):
    return jnp.concatenate([b[B * g : B * g + B] for b in blocks], axis=0)


def lanes(rows):
    return lax.broadcasted_iota(jnp.int32, (rows, 128), 1)


def pack_interp(interp_t):
    wide = jnp.concatenate([interp_t, jnp.zeros((R, 128 - S), f32)], axis=1)
    tail = wide[120:]
    side = jnp.concatenate([pltpu.roll(tail, 96, 1), pltpu.roll(tail, 64, 1), pltpu.roll(tail, 32, 1)], axis=0)
    return jnp.where(lanes(120) < S, wide[:120], side)


def unpack_interp(x):
    lane = lanes(40)
    tail = jnp.where(
        lane < 32,
        pltpu.roll(x[:40], 32, 1),
        jnp.where(lane < 64, pltpu.roll(x[40:80], 64, 1), pltpu.roll(x[80:120], 96, 1)),
    )
    return jnp.concatenate([x, tail], axis=0)[:, :S]


def pack_inverse(z):
    left, right = z[:, :128], z[:, 128:]
    lane = lanes(B)
    mixed = jnp.where(lane < 96, right[96:128], pltpu.roll(right[32:64], 96, 1))
    halves = jnp.where(lanes(16) < 64, right[64:80], pltpu.roll(right[80:96], 64, 1))
    lane = lanes(40)
    column = left[120:]
    for q in (2, 1, 0):
        column = jnp.where(lane < 32 * (q + 1), pltpu.roll(left[40 * q : 40 * q + 40], 32 * (q + 1), 1), column)
    return jnp.concatenate([right[128:160], mixed, halves, column], axis=0)


def unpack_inverse(x):
    lane = lanes(B)
    mixed = x[32:64]
    one = jnp.where(lane < 32, pltpu.roll(mixed, 32, 1), 0.0)
    three = jnp.where(lane < 96, mixed, 0.0)
    halves = x[64:80]
    two = jnp.concatenate([halves, pltpu.roll(halves, 64, 1)], axis=0)
    two = jnp.where(lane < 64, two, 0.0)
    right = jnp.concatenate([jnp.zeros((B, 128), f32), one, two, three, x[:32]], axis=0)
    column = x[80:120]
    left = jnp.concatenate([pltpu.roll(column, 96, 1), pltpu.roll(column, 64, 1), pltpu.roll(column, 32, 1), column], axis=0)
    left = jnp.where(lanes(R) < S, 0.0, left)
    return jnp.concatenate([left, right], axis=1)


def pack_symmetric(x, f=0):
    row = lax.broadcasted_iota(jnp.int32, (128, 128), 0)
    lane = lax.broadcasted_iota(jnp.int32, (128, 128), 1)
    upper, lower = x[:128, :128], x[128:, 128:]
    both = jnp.where(row >= lane, upper, lower)
    diag = jnp.sum(jnp.where(row == lane, lower, 0.0), axis=0, keepdims=True)
    diag = jnp.where(row[:8] == f, jnp.broadcast_to(diag, (8, 128)), 0.0)
    return jnp.concatenate([both, x[:128, 128:]], axis=1), jnp.concatenate([diag, diag], axis=1)


def unpack_symmetric(x, diag):
    row = lax.broadcasted_iota(jnp.int32, (128, 128), 0)
    lane = lax.broadcasted_iota(jnp.int32, (128, 128), 1)
    both, side = x[:, :128], x[:, 128:]
    turned = both.T
    upper = jnp.where(row >= lane, both, turned)
    diag = jnp.broadcast_to(diag[:, :128], (128, 128))
    lower = jnp.where(row < lane, both, jnp.where(row == lane, diag, turned))
    return jnp.concatenate(
        [jnp.concatenate([upper, side], axis=1), jnp.concatenate([side.T, lower], axis=1)], axis=0
    )


def update(near, interp_t, z):
    rest = near[S:] - nn3(interp_t, near[:S])
    p = nn3(z, jnp.concatenate([near[:S], rest], axis=0))
    pt = p.T
    return nt3(pt, pt)


def split_kernel(cx, xs):
    for f in range(NF):
        for i, piece in enumerate(split3(cx[f])):
            xs[f, i] = piece


def three(ref, f):
    return ref[f, 0], ref[f, 1], ref[f, 2]


def next_x_kernel(skel_x, xs, skel_y, dx, gx):
    for f in range(NF):
        x = choose(onehot(skel_x[f : f + 1, :]), three(xs, f), NT)
        dx[f] = x
        gx[f] = nt(x[:S], x)


def next_y_kernel(skel_y, cy, after, dy, gy):
    y = choose(onehot(skel_y[:1, :]), split3(cy[NF - 1]), NT)
    dy[0] = y
    gy[0] = nt(y[:S], y)


def local_kernel(skel, a, xs, cy, after, ex, ey, ap, dy, k_out):
    parts = [split3(cy[f]) for f in range(NF)]
    for f in range(NF):
        q = onehot(skel[f : f + 1, :])
        x = choose(q, three(xs, f))
        ex[f] = x
        y = choose(q, parts[f])
        ey[f] = y
        k = nt(x[:S], x) + nt(y[:S], y)
        if f:
            y = choose(q, parts[f - 1], NT)
            dy[f - 1] = y
            k = k + nt(y[:S], y)
        k_out[f] = k
        ap[f] = choose(q, split3(choose_columns(a[f], q)))


def interp_kernel(k_ref, gx, gy, interp_out, packed_out):
    grams = []
    rows = []
    for f in range(NF):
        k = k_ref[f] + gx[f]
        if f == 0:
            k = k + gy[0]
        grams.append(k[:, :128])
        rows.append(jnp.concatenate([k[:, :128].T, k[:, 128:].T], axis=0)[S:])
    done = eliminate([stack(grams, i) for i in range(S // B)], 0, NF, nn, nt)
    for f in range(NF):
        inv = unstack(done, f)[:, :S]
        interp_t = nn(nt(rows[f], inv), inv)
        interp_out[f] = interp_t
        packed_out[f] = pack_interp(interp_t)


def factor_kernel(ap, interp, z_out, packed_out, first_out):
    systems = []
    for f in range(NF):
        interp_t = interp[f]
        xr = ap[f, S:, :] - nn3(interp_t, ap[f, :S, :])
        t = xr[:, :S]
        systems.append(jnp.concatenate([t, xr[:, S:] - nt3(t, interp_t)], axis=1))
    done = eliminate([stack(systems, i) for i in range(R // B)], S, NF, nn3, nt3)
    for f in range(NF):
        z = unstack(done, f)
        z_out[f] = z
        packed = pack_inverse(z)
        packed_out[f] = packed
        if f == 0:
            first_out[0] = jnp.concatenate([packed, pack_interp(interp[0])], axis=0)


def inverse_of(z):
    return jnp.where(lax.broadcasted_iota(jnp.int32, (R, F), 1) < S, 0.0, z)


def plus_kernel(ex, ey, interp, z, interp_in, plus_x, plus_y):
    tail = jnp.zeros((8, F), f32)
    for f in range(NF):
        x, diag = pack_symmetric(update(ex[f], interp[f], inverse_of(z[f])), f)
        plus_x[128 * f : 128 * f + 128, :] = x
        tail = tail + diag
    plus_x[128 * NF :, :] = tail
    x, diag = pack_symmetric(update(ey[NF - 1], interp[NF - 1], inverse_of(z[NF - 1])))
    plus_y[:128, :] = x
    plus_y[128:, :] = diag


def inner_kernel(a, ey, dy, interp, z, ap, after, out, sk_out):
    inverses = [inverse_of(z[f]) for f in range(NF)]
    for f in range(NF):
        x = a[f]
        if f:
            x = x - update(ey[f - 1], interp[f - 1], inverses[f - 1])
        if f + 1 < NF:
            x = x - update(dy[f], interp[f + 1], inverses[f + 1])
        out[f] = x
        st = z[f, :, :128].T[:S]
        sk_out[f] = ap[f, :S, :S] - nt3(st, st)


def minus_kernel(part, dx, dy, interp, inverse, both, out):
    for f in range(NF):
        x = part[f] - update(dx[f], unpack_interp(interp[f]), unpack_inverse(inverse[f]))
        if f + 1 == NF:
            y = both[0]
            x = x - update(dy[0], unpack_interp(y[120:]), unpack_inverse(y[:120]))
        out[f] = x


def last_kernel(part, plus_x, plus_y, out):
    for f in range(NF):
        packed = plus_x[128 * f : 128 * f + 128, :]
        diag = plus_x[128 * NF + f : 128 * NF + f + 1, :]
        if f == 0:
            packed = packed + plus_y[:128, :]
            diag = diag + plus_y[128:129, :]
        out[f] = part[f] - unpack_symmetric(packed, diag)


def call(body, outs, count, unread=(), cost=1000):
    specs = [pl.BlockSpec(memory_space=pl.ANY if i in unread else pltpu.VMEM) for i in range(count)]
    return pl.pallas_call(
        body,
        out_shape=outs,
        in_specs=specs,
        compiler_params=pltpu.CompilerParams(vmem_limit_bytes=20 * 1024 * 1024),
        cost_estimate=pl.CostEstimate(flops=cost, bytes_accessed=1000, transcendentals=0),
    )


def arr(*shape):
    return jax.ShapeDtypeStruct(shape, f32)


def shifted(x, axis, distance):
    count = lax.axis_size(axis)
    return lax.ppermute(x, axis, [(i, (i + distance) % count) for i in range(count)])


def shards(face_matrix, couple_x, couple_y, skeleton, redundant):
    a, cx, cy, skel = face_matrix[0], couple_x[0], couple_y[0], skeleton[0]
    skel_x = shifted(skel, "gx", -1)
    skel_y = shifted(skel, "gy", -1)
    square = arr(NF, F, F)
    pieces = jax.ShapeDtypeStruct((NF, 3, F, F), bf16)
    xs = call(split_kernel, pieces, 1)(cx)
    dx, gx = call(next_x_kernel, (square, arr(NF, S, F)), 3, (2,))(skel_x, xs, skel_y)
    gx_in = shifted(gx, "gx", 1)
    dy_last, gy = call(next_y_kernel, (arr(1, F, F), arr(1, S, F)), 3, (2,))(skel_y, cy, gx)
    gy_in = shifted(gy, "gy", 1)
    ex, ey, ap, dy, k_loc = call(
        local_kernel, (square, square, square, arr(NF - 1, F, F), arr(NF, S, F)), 5, (4,)
    )(skel, a, xs, cy, gy)
    interp, interp_packed = call(interp_kernel, (arr(NF, R, S), arr(NF, 120, 128)), 3)(k_loc, gx_in, gy_in)
    interp_in = shifted(interp_packed, "gx", -1)
    z, z_packed, z_first = call(
        factor_kernel, (arr(NF, R, F), arr(NF, 120, 128), arr(1, 240, 128)), 2
    )(ap, interp)
    z_in = shifted(z_packed, "gx", -1)
    first_in = shifted(z_first, "gy", -1)
    plus_x, plus_y = call(plus_kernel, (arr(128 * NF + 8, F), arr(136, F)), 5, (4,))(ex, ey, interp, z, interp_in)
    plus_x_in = shifted(plus_x, "gx", 1)
    plus_y_in = shifted(plus_y, "gy", 1)
    part, sk = call(inner_kernel, (square, arr(NF, S, S)), 7, (6,))(a, ey, dy, interp, z, ap, plus_y)
    part = call(minus_kernel, square, 6, cost=MINUS)(part, dx, dy_last, interp_in, z_in, first_in)
    out = call(last_kernel, square, 3)(part, plus_x_in, plus_y_in)
    return out[None], sk[None]


def solution(mesh):
    spec4 = P("gx", "gy", None, None)
    spec3 = P("gx", "gy", None)
    return jax.shard_map(
        shards,
        mesh=mesh,
        in_specs=(spec4, spec4, spec4, spec3, spec3),
        out_specs=(spec4, spec4),
        check_vma=False,
    )
```
